32 devices in a mesh: groups: 2 (over x), space: 16 (over z, y, core).
Axes of the slice: x: 2, y: 2, z: 4, core: 2. Of those that a mesh axis runs over, the one named last changes fastest.
Arguments:
- conductivity: float32 [64, 256, 128], P('space', 'groups'), parts along dimension 1, may hold values from 0.3 to 3
- forward: float32 [16, 64, 128, 128], P('groups', 'space'), parts along dimension 0, may hold values from -6 to 6
- adjoint_rhs: float32 [16, 64, 128, 128], P('groups', 'space'), parts along dimension 0, may hold values from -6 to 6
- plane_counts: int32 [32], P('groups'), parts along dimension 0, may hold values from 1 to 4, 32 in all
Outputs:
- adjoint: float32 [16, 64, 128, 128], P('groups', 'space'), parts along dimension 0
- gradient: float32 [64, 256, 128], P('space', 'groups'), parts along dimension 1
The draws below stay inside these ranges and needn't reach their ends.
There are 2 independent parts, one for each index of `groups`. The reference program is written for one: setup_inputs(seed, part) draws one part's arguments, and reference() takes and returns one part's arrays. A program takes and returns all parts, laid end to end along the dimension named above; each array names one. Nothing has to cross between parts.
Inputs may be any that keep to these rules, and one draw needn't show every extreme that they name: `plane_counts`: they sum to 32, and the largest is exactly 4.
All inputs are finite; a program needn't handle non-finite values.
Results may differ from the reference program's by a relative error of at most 0.0001.
Values sent between devices are 32-bit elements; how exact they have to be, the bound alone decides.
A program may use at most 128 MiB of HBM per device.

```python
import math
import jax
import jax.numpy as jnp
import numpy as np

NY = 128
NZ = 128
SRC = 8
NU = 2
NC = 4
CYCLES = 2
CAP = 4
SLABS = 16
NX = 32
SLOTS = 64


def shard_levels(stream_key, extent, shards, low, largest):
    factor_of = 1.0
    for dim, blocks in shards:
        draws = jax.random.uniform(jax.random.fold_in(jax.random.fold_in(stream_key, 6), dim), (blocks,), jnp.float32, low / len(shards), largest / len(shards))
        factor_of = factor_of * jnp.repeat(jnp.exp(draws), extent[dim] // blocks).reshape((-1,) + (1,) * (len(extent) - 1 - dim))
    return factor_of


def profile(count, total, bound, lean):
    weights = [(1 << 20) // math.isqrt(grade ** lean) + 1 for grade in range(2, count + 1)]
    spare, holding = total - bound - (count - 1), [1] * (count - 1)
    while spare > 0:
        movable = [i for i in range(count - 1) if holding[i] < bound]
        mass, remaining = sum([weights[i] for i in movable]), spare
        for i in movable:
            extra = min(bound - holding[i], max(1, remaining * weights[i] // mass), spare)
            holding[i] = holding[i] + extra
            spare = spare - extra
    return np.array([bound] + holding)


def ragged(key, number_of, total, limit, lean):
    if number_of == 2:
        one = jax.random.randint(key, (), max(1, total - limit), min(limit, total - 1) + 1)
        return jnp.stack([one, total - one])
    lengths = jnp.asarray(profile(number_of, total, limit, lean), jnp.int32)
    pairs = (number_of - 1) // 2
    giver, taker = lengths[1:1 + 2 * pairs:2], lengths[2:2 + 2 * pairs:2]
    slack = jnp.minimum(giver - 1, limit - taker)
    moved = jax.random.randint(jax.random.fold_in(key, 1), (pairs,), 0, 1 << 20) % (slack + 1)
    lengths = lengths.at[1:1 + 2 * pairs:2].set(giver - moved).at[2:2 + 2 * pairs:2].set(taker + moved)
    return lengths[jax.random.permutation(jax.random.fold_in(key, 2), number_of)]


def bell_draw(key, dims, scale, most, split=(), kind=jnp.bfloat16):
    array = jax.random.normal(key, dims, jnp.float32) * scale
    if len(split) > 0:
        array = shard_levels(key, dims, split, -0.22, 0.18) * array
    return jnp.clip(array, min=-most, max=most).astype(kind)


def setup_inputs(seed: int = 0, part: int = 0) -> dict:
    seeds = jax.random.split(jax.random.key(seed), 5)
    part_keys = jax.random.split(jax.random.fold_in(seeds[4], part), 5)
    return {
        "conductivity": jnp.clip(jnp.exp(math.log(3.0) - 2.3025851 * jax.random.uniform(part_keys[0], (SLOTS, NY, NZ), jnp.float32) ** shard_levels(part_keys[0], (SLOTS, NY, NZ), ((0, 16),), -0.2, 0.2)), 0.3, 3.0),
        "forward": bell_draw(part_keys[1], (SRC, SLOTS, NY, NZ), 1.0, 6.0, ((1, 16),), jnp.float32),
        "adjoint_rhs": bell_draw(part_keys[2], (SRC, SLOTS, NY, NZ), 1.0, 6.0, ((1, 16),), jnp.float32),
        "plane_counts": ragged(part_keys[3], SLABS, NX, CAP, 2).astype(jnp.int32),
    }


OMEGA = 0.8


def compact_index(plane_counts):
    plane_ends = jnp.cumsum(plane_counts).astype(jnp.int32)
    plane_starts = (plane_ends - plane_counts).astype(jnp.int32)
    plane_ids = jnp.arange(NX, dtype=jnp.int32)
    owner_rank = jnp.sum((plane_ends[None, :] <= plane_ids[:, None]).astype(jnp.int32), axis=1).astype(jnp.int32)
    return (owner_rank * CAP + plane_ids - plane_starts[owner_rank]).astype(jnp.int32)


def neighbors(values):
    padded = jnp.pad(values, ((0, 0), (1, 1), (1, 1), (1, 1)))
    return [padded[:, :-2, 1:-1, 1:-1], padded[:, 2:, 1:-1, 1:-1], padded[:, 1:-1, :-2, 1:-1],
            padded[:, 1:-1, 2:, 1:-1], padded[:, 1:-1, 1:-1, :-2], padded[:, 1:-1, 1:-1, 2:]]


def face_values(conduct, neighbor_list, x_weight):
    weights = [x_weight, x_weight, 1.0, 1.0, 1.0, 1.0]
    return [(conduct + neighbor_list[position]) * 0.5 * weights[position] for position in range(6)]


def total_of(terms_list):
    accum = terms_list[0]
    for position in range(1, len(terms_list)):
        accum = accum + terms_list[position]
    return accum


def apply_op(values, face_list, neighbor_list):
    return total_of([face_list[position] * (values - neighbor_list[position]) for position in range(6)])


def relax(values, source_term, face_list, diagonal):
    image = apply_op(values, face_list, neighbors(values))
    return values + OMEGA * (source_term - image) / diagonal


def block_sum(values):
    shape = values.shape
    return values.reshape(shape[0], shape[1], shape[2] // 4, 4, shape[3] // 4, 4).sum(axis=(3, 5))


def block_mean(values):
    shape = values.shape
    return values.reshape(shape[0], shape[1], shape[2] // 4, 4, shape[3] // 4, 4).mean(axis=(3, 5))


def expand(values):
    return jnp.repeat(jnp.repeat(values, 4, axis=2), 4, axis=3)


def reference(conductivity, forward, adjoint_rhs, plane_counts):
    order = compact_index(plane_counts)
    conduct = jnp.take(conductivity, order, axis=0)[None]
    fields = jnp.take(forward, order, axis=1)
    source_term = jnp.take(adjoint_rhs, order, axis=1)
    fine_faces = face_values(conduct, neighbors(conduct), 1.0)
    fine_diag = total_of(fine_faces)
    coarse_conduct = block_mean(conduct)
    coarse_faces = face_values(coarse_conduct, neighbors(coarse_conduct), 16.0)
    coarse_diag = total_of(coarse_faces)
    adjoint = jnp.zeros(source_term.shape, jnp.float32)
    for cycle_index in range(CYCLES):
        for sweep_index in range(NU):
            adjoint = relax(adjoint, source_term, fine_faces, fine_diag)
        residue = source_term - apply_op(adjoint, fine_faces, neighbors(adjoint))
        coarse_res = block_sum(residue)
        correction = jnp.zeros(coarse_res.shape, jnp.float32)
        for sweep_index in range(NC):
            correction = relax(correction, coarse_res, coarse_faces, coarse_diag)
        adjoint = adjoint + expand(correction)
        for sweep_index in range(NU):
            adjoint = relax(adjoint, source_term, fine_faces, fine_diag)
    near_fwd = neighbors(fields)
    near_adj = neighbors(adjoint)
    products = total_of([(fields - near_fwd[position]) * (adjoint - near_adj[position]) for position in range(6)])
    grad_field = -0.5 * jnp.sum(products, axis=0)
    adjoint_out = jnp.zeros((SRC, SLOTS, NY, NZ), jnp.float32).at[:, order].set(adjoint)
    grad_out = jnp.zeros((SLOTS, NY, NZ), jnp.float32).at[order].set(grad_field)
    return adjoint_out, grad_out
```

```python
import functools

import jax
import jax.numpy as jnp
from jax import lax
from jax.experimental import pallas as pl
from jax.experimental.pallas import tpu as pltpu
from jax.sharding import PartitionSpec as P

OMEGA = 0.8
F32 = jnp.float32
PAD = 8
RB = 32
CH = 2
STEPS = 8
CSTEPS = 8


def dot(a, b):
    return jnp.dot(a, b, precision=lax.Precision.HIGHEST, preferred_element_type=F32)


def kernel(n_ref, cond, fwd, rhs, adj, grad,
           w, dg, bs, va, vb, hlo, hhi, sup, sdn, fhlo, fhhi, fsup, fsdn,
           qm, qt, cw, cwb, cres, cbs, ce, chlo, chhi, csup, csdn,
           kup, kdn, klo, khi, plo, phi, rlo, rhi, sy, sz, sfa, sx, rbuf,
           up_send, up_recv, dn_send, dn_recv, cup_send, cup_recv, cdn_send, cdn_recv,
           mup_send, mup_recv, mdn_send, mdn_recv):
    slots, ny, nz = cond.shape
    nsrc = fwd.shape[0]
    half = nsrc // 2
    chunks = nsrc // CH
    cy = ny // 4
    pos = lax.axis_index("space")
    peers = lax.axis_size("space")
    n = n_ref[0]
    top = jnp.maximum(n - 1, 0)
    has_lo = pos > 0
    has_hi = pos < peers - 1

    def up_copy(src, dst, ss, rs):
        return pltpu.make_async_remote_copy(
            src_ref=src, dst_ref=dst, send_sem=ss, recv_sem=rs,
            device_id={"space": pos + 1}, device_id_type=pl.DeviceIdType.MESH)

    def dn_copy(src, dst, ss, rs):
        return pltpu.make_async_remote_copy(
            src_ref=src, dst_ref=dst, send_sem=ss, recv_sem=rs,
            device_id={"space": pos - 1}, device_id_type=pl.DeviceIdType.MESH)

    barrier = pltpu.get_barrier_semaphore()

    @pl.when(has_lo)
    def _():
        pl.semaphore_signal(barrier, inc=1, device_id={"space": pos - 1},
                            device_id_type=pl.DeviceIdType.MESH)

    @pl.when(has_hi)
    def _():
        pl.semaphore_signal(barrier, inc=1, device_id={"space": pos + 1},
                            device_id_type=pl.DeviceIdType.MESH)

    pl.semaphore_wait(barrier, jnp.where(has_lo, 1, 0) + jnp.where(has_hi, 1, 0))

    def fine(step, c):
        part = pl.ds(c * CH, CH)
        return (lambda: up_copy(sup.at[step, part], hlo.at[step, part],
                                up_send.at[step, c], up_recv.at[step, c]),
                lambda: dn_copy(sdn.at[step, part], hhi.at[step, part],
                                dn_send.at[step, c], dn_recv.at[step, c]))

    def coarse(k):
        return (lambda: up_copy(csup.at[k], chlo.at[k], cup_send.at[k], cup_recv.at[k]),
                lambda: dn_copy(csdn.at[k], chhi.at[k], cdn_send.at[k], cdn_recv.at[k]))

    def misc(i, us, ud, ds, dd):
        return (lambda: up_copy(us, ud, mup_send.at[i], mup_recv.at[i]),
                lambda: dn_copy(ds, dd, mdn_send.at[i], mdn_recv.at[i]))

    cond_pair = misc(0, kup, klo, kdn, khi)
    fwd_pair = misc(1, fsup, fhlo, fsdn, fhhi)
    prod_pair = misc(2, phi, rlo, plo, rhi)

    def start(pair, up=True, dn=True):
        if up:
            @pl.when(has_hi)
            def _():
                pair[0]().start()
        if dn:
            @pl.when(has_lo)
            def _():
                pair[1]().start()

    def wait_recv(pair, up=True, dn=True):
        if up:
            @pl.when(has_lo)
            def _():
                pair[0]().wait_recv()
        if dn:
            @pl.when(has_hi)
            def _():
                pair[1]().wait_recv()

    def wait_send(pair, up=True, dn=True):
        if up:
            @pl.when(has_hi)
            def _():
                pair[0]().wait_send()
        if dn:
            @pl.when(has_lo)
            def _():
                pair[1]().wait_send()

    kup[...] = cond[top]
    kdn[...] = cond[0]
    start(cond_pair)

    plane = jnp.zeros((ny, nz), F32)

    @pl.when(jnp.logical_not(has_lo))
    def _():
        klo[...] = plane
        chlo[...] = jnp.zeros_like(chlo)
        fhlo[...] = jnp.zeros_like(fhlo)

        @pl.loop(0, STEPS)
        def _(k):
            hlo[k] = jnp.zeros(hlo.shape[1:], F32)

    @pl.when(jnp.logical_not(has_hi))
    def _():
        khi[...] = plane
        chhi[...] = jnp.zeros_like(chhi)
        fhhi[...] = jnp.zeros_like(fhhi)

        @pl.loop(0, STEPS)
        def _(k):
            hhi[k] = jnp.zeros(hhi.shape[1:], F32)

    edge = jnp.zeros((slots, PAD, nz), F32)

    @pl.loop(0, nsrc)
    def _(s):
        for buf in (bs, va, vb):
            buf[s, :, :PAD] = edge
            buf[s, :, PAD + ny:] = edge

    row = lax.broadcasted_iota(jnp.int32, (ny, nz), 0)
    lane = lax.broadcasted_iota(jnp.int32, (ny, nz), 1)
    for s4 in range(4):
        qm[s4] = jnp.where(row // 4 + 32 * s4 == lane, 1.0, 0.0).astype(F32)
        qt[s4] = jnp.where(lane // 4 + 32 * s4 == row, 1.0, 0.0).astype(F32)

    @pl.loop(0, half)
    def _(s):
        fsup[s] = fwd[s, top]
        fsdn[s] = fwd[half + s, 0]

    wait_recv(cond_pair)

    for j in range(slots):
        c = cond[j]
        lo = klo[...] if j == 0 else cond[j - 1]
        above = plane if j == slots - 1 else cond[j + 1]
        hi = jnp.where(n - 1 == j, khi[...], above)
        faces = [(c + lo) * 0.5, (c + hi) * 0.5,
                 (c + jnp.where(row == 0, 0.0, pltpu.roll(c, 1, 0))) * 0.5,
                 (c + jnp.where(row == ny - 1, 0.0, pltpu.roll(c, ny - 1, 0))) * 0.5,
                 (c + jnp.where(lane == 0, 0.0, pltpu.roll(c, 1, 1))) * 0.5,
                 (c + jnp.where(lane == nz - 1, 0.0, pltpu.roll(c, nz - 1, 1))) * 0.5]
        diag = faces[0] + faces[1] + faces[2] + faces[3] + faces[4] + faces[5]
        alive = jnp.where(j < n, 1.0, 0.0)
        scale = alive * (OMEGA / diag)
        dg[j] = alive * diag * (1.0 / OMEGA)
        for i in range(4):
            w[i, j] = scale * faces[i]
        w[4, j] = jnp.where(lane == 0, 0.0, scale * faces[4])
        w[5, j] = jnp.where(lane == nz - 1, 0.0, scale * faces[5])
        w[6, j] = scale

    def stage(step, s, buf, off):
        sup[step, s] = buf[s, top, off:off + ny]
        sdn[step, s] = buf[s, 0, off:off + ny]

    @pl.loop(0, chunks)
    def _(c):
        for i in range(CH):
            s = c * CH + i
            for j in range(slots):
                bs[s, j, PAD:PAD + ny] = w[6, j] * rhs[s, j]
            stage(0, s, bs, PAD)
        start(fine(0, c))

    qall = jnp.where(row // 4 == lane % 32, 1.0 / 16.0, 0.0).astype(F32)

    def rows4(read):
        return read(0) + read(1) + read(2) + read(3)

    def every4(k):
        return pl.ds(k, cy, stride=4)

    cplanes = [rows4(lambda k, j=j: cond[j, every4(k), :]) for j in range(slots)]
    cplanes += [rows4(lambda k: klo[every4(k), :]), rows4(lambda k: khi[every4(k), :])]
    cmean = dot(jnp.concatenate(cplanes, axis=0), qall)
    cc = [cmean[j * cy:(j + 1) * cy] for j in range(slots + 2)]
    crow = lax.broadcasted_iota(jnp.int32, (cy, nz), 0)
    clane = lax.broadcasted_iota(jnp.int32, (cy, nz), 1) % 32
    for j in range(slots):
        c = cc[j]
        lo = cc[slots] if j == 0 else cc[j - 1]
        hi = jnp.where(n - 1 == j, cc[slots + 1], jnp.zeros_like(c) if j == slots - 1 else cc[j + 1])
        faces = [(c + lo) * 8.0, (c + hi) * 8.0,
                 (c + jnp.where(crow == 0, 0.0, pltpu.roll(c, 1, 0))) * 0.5,
                 (c + jnp.where(crow == cy - 1, 0.0, pltpu.roll(c, cy - 1, 0))) * 0.5,
                 (c + jnp.where(clane == 0, 0.0, pltpu.roll(c, 1, 1))) * 0.5,
                 (c + jnp.where(clane == 31, 0.0, pltpu.roll(c, nz - 1, 1))) * 0.5]
        diag = faces[0] + faces[1] + faces[2] + faces[3] + faces[4] + faces[5]
        scale = jnp.where(j < n, 1.0, 0.0) * (OMEGA / diag)
        cw[0, j] = scale * faces[0]
        cw[1, j] = scale * faces[1]
        cw[2, j] = jnp.where(crow == 0, 0.0, scale * faces[2])
        cw[3, j] = jnp.where(crow == cy - 1, 0.0, scale * faces[3])
        cw[4, j] = jnp.where(clane == 0, 0.0, scale * faces[4])
        cw[5, j] = jnp.where(clane == 31, 0.0, scale * faces[5])
        cwb[pl.ds(j * cy, cy), :] = scale

    def change(src, step, s, j, r0, wts, keep):
        o = PAD + r0
        rows = slice(o, o + RB)
        v = src[s, j, rows]
        lo = hlo[step, s, r0:r0 + RB] if j == 0 else src[s, j - 1, rows]
        edge_hi = hhi[step, s, r0:r0 + RB]
        above = jnp.zeros_like(edge_hi) if j == slots - 1 else src[s, j + 1, rows]
        hi = jnp.where(n - 1 == j, edge_hi, above)
        acc = bs[s, j, rows] + keep * v
        acc = acc + wts[0] * lo + wts[1] * hi
        acc = acc + wts[2] * src[s, j, o - 1:o - 1 + RB] + wts[3] * src[s, j, o + 1:o + 1 + RB]
        return acc + wts[4] * pltpu.roll(v, 1, 1) + wts[5] * pltpu.roll(v, nz - 1, 1)

    def weights(j, r0):
        return [w[i, j, r0:r0 + RB] for i in range(6)]

    def sweep(src, dst, off, step, prepare=None):
        @pl.loop(0, chunks)
        def _(c):
            if prepare is None:
                wait_recv(fine(step, c))
            else:
                prepare(c)
            for j in range(slots):
                for r0 in range(0, ny, RB):
                    wts = weights(j, r0)
                    for i in range(CH):
                        s = c * CH + i
                        dst[s, j, off + r0:off + r0 + RB] = change(
                            src, step, s, j, r0, wts, 1.0 - OMEGA)
            for i in range(CH):
                stage(step + 1, c * CH + i, dst, off)
            if step + 1 < STEPS - 1:
                start(fine(step + 1, c))
            else:
                first = c < chunks // 2

                @pl.when(first)
                def _():
                    start(fine(step + 1, c), dn=False)

                @pl.when(jnp.logical_not(first))
                def _():
                    start(fine(step + 1, c), up=False)

    def coarse_solve(src, step, k0):
        cres[...] = jnp.zeros_like(cres)

        @pl.loop(0, chunks)
        def _(c):
            wait_recv(fine(step, c))
            g = c // 2
            for i in range(CH):
                s = c * CH + i
                for j in range(slots):
                    for r0 in range(0, ny, RB):
                        rbuf[i, j, r0:r0 + RB] = dg[j, r0:r0 + RB] * change(
                            src, step, s, j, r0, weights(j, r0), -OMEGA)
                sums = [rows4(lambda k, j=j: rbuf[i, j, every4(k), :]) for j in range(slots)]
                cres[g] = cres[g] + dot(jnp.concatenate(sums, axis=0), qm[(c % 2) * CH + i])

        for g in range(2):
            first = cwb[...] * cres[g]
            for j in range(slots):
                cbs[g, j] = first[j * cy:(j + 1) * cy]
        for t in range(4):
            here = cbs if t == 0 else ce.at[t - 1]
            for g in range(2):
                csup[k0 + t, g] = here[g, top]
                csdn[k0 + t, g] = here[g, 0]
            start(coarse(k0 + t))
            if t < 3:
                wait_recv(coarse(k0 + t))
                for g in range(2):
                    for j in range(slots):
                        e = here[g, j]
                        lo = chlo[k0 + t, g] if j == 0 else here[g, j - 1]
                        above = jnp.zeros_like(e) if j == slots - 1 else here[g, j + 1]
                        hi = jnp.where(n - 1 == j, chhi[k0 + t, g], above)
                        ce[t, g, j] = (
                            cbs[g, j] + (1.0 - OMEGA) * e + cw[0, j] * lo + cw[1, j] * hi
                            + cw[2, j] * pltpu.roll(e, 1, 0) + cw[3, j] * pltpu.roll(e, cy - 1, 0)
                            + cw[4, j] * pltpu.roll(e, 1, 1) + cw[5, j] * pltpu.roll(e, nz - 1, 1))
        last = ce.at[2]
        wait_recv(coarse(k0 + 3))

        def add_correction(c):
            g = c // 2
            packed = jnp.concatenate(
                [last[g, j] for j in range(slots)] + [chlo[k0 + 3, g], chhi[k0 + 3, g]], axis=0)
            for i in range(CH):
                s = c * CH + i
                wide = dot(packed, qt[(c % 2) * CH + i])
                for k in range(4):
                    for j in range(slots):
                        at = pl.ds(PAD + k, cy, stride=4)
                        src[s, j, at, :] = src[s, j, at, :] + wide[j * cy:(j + 1) * cy]
                    at = every4(k)
                    hlo[step, s, at, :] = hlo[step, s, at, :] + wide[slots * cy:(slots + 1) * cy]
                    hhi[step, s, at, :] = hhi[step, s, at, :] + wide[(slots + 1) * cy:]

        return add_correction

    sweep(bs, va, PAD, 0)
    start(fwd_pair)
    correct = coarse_solve(va, 1, 0)
    sweep(va, vb, PAD, 1, correct)
    sweep(vb, va, PAD, 2)
    sweep(va, vb, PAD, 3)
    sweep(vb, va, PAD, 4)
    correct = coarse_solve(va, 5, 4)
    sweep(va, vb, PAD, 5, correct)
    sweep(vb, adj, 0, 6)

    zero = jnp.zeros_like(sy)
    sy[...] = zero
    sz[...] = zero
    sfa[...] = zero
    sx[...] = zero

    @pl.loop(0, nsrc)
    def _(s):
        for j in range(slots):
            f, a = fwd[s, j], adj[s, j]
            sfa[j] = sfa[j] + f * a
            sy[j] = sy[j] + ((f - jnp.where(row == 0, 0.0, pltpu.roll(f, 1, 0)))
                             * (a - jnp.where(row == 0, 0.0, pltpu.roll(a, 1, 0))))
            sz[j] = sz[j] + ((f - jnp.where(lane == 0, 0.0, pltpu.roll(f, 1, 1)))
                             * (a - jnp.where(lane == 0, 0.0, pltpu.roll(a, 1, 1))))
            if j > 0:
                sx[j] = sx[j] + (f - fwd[s, j - 1]) * (a - adj[s, j - 1])

    wait_recv(fwd_pair)
    for c in range(chunks):
        wait_recv(fine(STEPS - 1, c), up=c < chunks // 2, dn=c >= chunks // 2)
    lower, upper = plane, plane
    for s in range(half):
        lower = lower + (fwd[s, 0] - fhlo[s]) * (adj[s, 0] - hlo[STEPS - 1, s])
    plo[...] = lower
    for s in range(half):
        upper = upper + ((fwd[half + s, top] - fhhi[s])
                         * (adj[half + s, top] - hhi[STEPS - 1, half + s]))
    phi[...] = upper
    start(prod_pair)

    @pl.when(jnp.logical_not(has_lo))
    def _():
        total = plane
        for s in range(half, nsrc):
            total = total + fwd[s, 0] * adj[s, 0]
        rlo[...] = total

    @pl.when(jnp.logical_not(has_hi))
    def _():
        total = plane
        for s in range(half):
            total = total + fwd[s, top] * adj[s, top]
        rhi[...] = total

    for j in range(slots):
        y_hi = jnp.where(row == ny - 1, sfa[j], pltpu.roll(sy[j], ny - 1, 0))
        z_hi = jnp.where(lane == nz - 1, sfa[j], pltpu.roll(sz[j], nz - 1, 1))
        sy[j] = sy[j] + y_hi + sz[j] + z_hi
    wait_recv(prod_pair)
    for j in range(slots):
        x_lo = plo[...] + rlo[...] if j == 0 else sx[j]
        x_hi = jnp.where(n - 1 == j, phi[...] + rhi[...], plane if j == slots - 1 else sx[j + 1])
        grad[j] = jnp.where(j < n, -0.5, 0.0) * (sy[j] + x_lo + x_hi)

    @pl.loop(0, STEPS - 1)
    def _(k):
        for c in range(chunks):
            wait_send(fine(k, c))
    for c in range(chunks):
        wait_send(fine(STEPS - 1, c), up=c < chunks // 2, dn=c >= chunks // 2)

    @pl.loop(0, CSTEPS)
    def _(k):
        wait_send(coarse(k))
    for pair in (cond_pair, fwd_pair, prod_pair):
        wait_send(pair)


def shards(conductivity, forward, adjoint_rhs, plane_counts):
    slots, ny, nz = conductivity.shape
    nsrc = forward.shape[0]
    half, chunks, cy = nsrc // 2, nsrc // CH, ny // 4
    n = lax.dynamic_slice(plane_counts, (lax.axis_index("space"),), (1,))
    vmem = functools.partial(pl.BlockSpec, memory_space=pltpu.VMEM)

    def buf(*shape):
        return pltpu.VMEM(shape, F32)

    def sems(*shape):
        return pltpu.SemaphoreType.DMA(shape)

    field = (nsrc, slots, ny + 2 * PAD, nz)
    scratch = [
        buf(7, slots, ny, nz), buf(slots, ny, nz), buf(*field), buf(*field), buf(*field),
        *[buf(STEPS, nsrc, ny, nz)] * 4,
        *[buf(half, ny, nz)] * 4,
        buf(4, nz, nz), buf(4, nz, nz),
        buf(6, slots, cy, nz), buf(slots * cy, nz), buf(2, slots * cy, nz),
        buf(2, slots, cy, nz), buf(3, 2, slots, cy, nz),
        *[buf(CSTEPS, 2, cy, nz)] * 4,
        *[buf(ny, nz)] * 8,
        *[buf(slots, ny, nz)] * 4,
        buf(CH, slots, ny, nz),
        *[sems(STEPS, chunks)] * 4,
        *[sems(CSTEPS)] * 4,
        *[sems(3)] * 4,
    ]
    return pl.pallas_call(
        kernel,
        out_shape=(jax.ShapeDtypeStruct(forward.shape, F32),
                   jax.ShapeDtypeStruct(conductivity.shape, F32)),
        in_specs=[pl.BlockSpec(memory_space=pltpu.SMEM), vmem(), vmem(), vmem()],
        out_specs=(vmem(), vmem()),
        scratch_shapes=scratch,
        compiler_params=pltpu.CompilerParams(
            collective_id=0, has_side_effects=True, vmem_limit_bytes=56 * 2**20),
    )(n, conductivity, forward, adjoint_rhs)


def solution(mesh):
    in_specs = (
        P("space", "groups", None),
        P("groups", "space", None, None),
        P("groups", "space", None, None),
        P("groups"),
    )
    out_specs = (P("groups", "space", None, None), P("space", "groups", None))
    return jax.shard_map(shards, mesh=mesh, in_specs=in_specs, out_specs=out_specs, check_vma=False)
```

```python
import functools

import jax
import jax.numpy as jnp
from jax import lax
from jax.experimental import pallas as pl
from jax.experimental.pallas import tpu as pltpu
from jax.sharding import PartitionSpec as P

OMEGA = 0.8
F32 = jnp.float32
PAD = 8
RB = 32
CH = 2
STEPS = 8
CSTEPS = 10


def dot(a, b):
    return jnp.dot(a, b, precision=lax.Precision.HIGHEST, preferred_element_type=F32)


def kernel(n_ref, cond, fwd, rhs, adj, grad,
           w, dg, bs, va, vb, hlo, hhi, sup, sdn, fhlo, fhhi, fsup, fsdn,
           qm, qt, cw, cwb, cres, cbs, ce, chlo, chhi, csup, csdn,
           kup, kdn, klo, khi, plo, phi, rlo, rhi, sy, sz, sfa, sx, rbuf, fx, ebuf,
           up_send, up_recv, dn_send, dn_recv, cup_send, cup_recv, cdn_send, cdn_recv,
           mup_send, mup_recv, mdn_send, mdn_recv):
    slots, ny, nz = cond.shape
    nsrc = fwd.shape[0]
    half = nsrc // 2
    chunks = nsrc // CH
    cy = ny // 4
    pos = lax.axis_index("space")
    peers = lax.axis_size("space")
    n = n_ref[pos]
    top = jnp.maximum(n - 1, 0)
    has_lo = pos > 0
    has_hi = pos < peers - 1

    def up_copy(src, dst, ss, rs):
        return pltpu.make_async_remote_copy(
            src_ref=src, dst_ref=dst, send_sem=ss, recv_sem=rs,
            device_id={"space": pos + 1}, device_id_type=pl.DeviceIdType.MESH)

    def dn_copy(src, dst, ss, rs):
        return pltpu.make_async_remote_copy(
            src_ref=src, dst_ref=dst, send_sem=ss, recv_sem=rs,
            device_id={"space": pos - 1}, device_id_type=pl.DeviceIdType.MESH)

    barrier = pltpu.get_barrier_semaphore()

    @pl.when(has_lo)
    def _():
        pl.semaphore_signal(barrier, inc=1, device_id={"space": pos - 1},
                            device_id_type=pl.DeviceIdType.MESH)

    @pl.when(has_hi)
    def _():
        pl.semaphore_signal(barrier, inc=1, device_id={"space": pos + 1},
                            device_id_type=pl.DeviceIdType.MESH)

    pl.semaphore_wait(barrier, jnp.where(has_lo, 1, 0) + jnp.where(has_hi, 1, 0))

    def fine(step, c):
        part = pl.ds(c * CH, CH)
        return (lambda: up_copy(sup.at[step, part], hlo.at[step, part],
                                up_send.at[step, c], up_recv.at[step, c]),
                lambda: dn_copy(sdn.at[step, part], hhi.at[step, part],
                                dn_send.at[step, c], dn_recv.at[step, c]))

    def coarse(k):
        return (lambda: up_copy(csup.at[k], chlo.at[k], cup_send.at[k], cup_recv.at[k]),
                lambda: dn_copy(csdn.at[k], chhi.at[k], cdn_send.at[k], cdn_recv.at[k]))

    def misc(i, us, ud, ds, dd):
        return (lambda: up_copy(us, ud, mup_send.at[i], mup_recv.at[i]),
                lambda: dn_copy(ds, dd, mdn_send.at[i], mdn_recv.at[i]))

    cond_pair = misc(0, kup, klo, kdn, khi)
    fwd_pair = misc(1, fsup, fhlo, fsdn, fhhi)
    prod_pair = misc(2, phi, rlo, plo, rhi)

    def start(pair, up=True, dn=True):
        if up:
            @pl.when(has_hi)
            def _():
                pair[0]().start()
        if dn:
            @pl.when(has_lo)
            def _():
                pair[1]().start()

    def wait_recv(pair, up=True, dn=True):
        if up:
            @pl.when(has_lo)
            def _():
                pair[0]().wait_recv()
        if dn:
            @pl.when(has_hi)
            def _():
                pair[1]().wait_recv()

    def wait_send(pair, up=True, dn=True):
        if up:
            @pl.when(has_hi)
            def _():
                pair[0]().wait_send()
        if dn:
            @pl.when(has_lo)
            def _():
                pair[1]().wait_send()

    kup[...] = cond[top]
    kdn[...] = cond[0]
    start(cond_pair)

    plane = jnp.zeros((ny, nz), F32)

    @pl.when(jnp.logical_not(has_lo))
    def _():
        klo[...] = plane
        chlo[...] = jnp.zeros_like(chlo)
        fhlo[...] = jnp.zeros_like(fhlo)

        @pl.loop(0, STEPS)
        def _(k):
            hlo[k] = jnp.zeros(hlo.shape[1:], F32)

    @pl.when(jnp.logical_not(has_hi))
    def _():
        khi[...] = plane
        chhi[...] = jnp.zeros_like(chhi)
        fhhi[...] = jnp.zeros_like(fhhi)

        @pl.loop(0, STEPS)
        def _(k):
            hhi[k] = jnp.zeros(hhi.shape[1:], F32)

    edge = jnp.zeros((slots, PAD, nz), F32)

    @pl.loop(0, nsrc)
    def _(s):
        for buf in (bs, va, vb):
            buf[s, :, :PAD] = edge
            buf[s, :, PAD + ny:] = edge

    row = lax.broadcasted_iota(jnp.int32, (ny, nz), 0)
    lane = lax.broadcasted_iota(jnp.int32, (ny, nz), 1)
    for s4 in range(4):
        qm[s4] = jnp.where(row // 4 + 32 * s4 == lane, 1.0, 0.0).astype(F32)
        qt[s4] = jnp.where(lane // 4 + 32 * s4 == row, 1.0, 0.0).astype(F32)

    @pl.loop(0, half)
    def _(s):
        fsup[s] = fwd[s, top]
        fsdn[s] = fwd[half + s, 0]

    wait_recv(cond_pair)
    fx[0] = (cond[top] + khi[...]) * 0.5
    fx[1] = (cond[0] + klo[...]) * 0.5

    for j in range(slots):
        c = cond[j]
        lo = klo[...] if j == 0 else cond[j - 1]
        above = plane if j == slots - 1 else cond[j + 1]
        hi = jnp.where(n - 1 == j, khi[...], above)
        faces = [(c + lo) * 0.5, (c + hi) * 0.5,
                 (c + jnp.where(row == 0, 0.0, pltpu.roll(c, 1, 0))) * 0.5,
                 (c + jnp.where(row == ny - 1, 0.0, pltpu.roll(c, ny - 1, 0))) * 0.5,
                 (c + jnp.where(lane == 0, 0.0, pltpu.roll(c, 1, 1))) * 0.5,
                 (c + jnp.where(lane == nz - 1, 0.0, pltpu.roll(c, nz - 1, 1))) * 0.5]
        diag = faces[0] + faces[1] + faces[2] + faces[3] + faces[4] + faces[5]
        alive = jnp.where(j < n, 1.0, 0.0)
        scale = alive * (OMEGA / diag)
        dg[j] = alive * diag * (1.0 / OMEGA)
        for i in range(4):
            w[i, j] = scale * faces[i]
        w[4, j] = jnp.where(lane == 0, 0.0, scale * faces[4])
        w[5, j] = jnp.where(lane == nz - 1, 0.0, scale * faces[5])
        w[6, j] = scale

    def stage(step, s, buf, off):
        sup[step, s] = buf[s, top, off:off + ny]
        sdn[step, s] = buf[s, 0, off:off + ny]

    @pl.loop(0, chunks)
    def _(c):
        for i in range(CH):
            s = c * CH + i
            for j in range(slots):
                bs[s, j, PAD:PAD + ny] = w[6, j] * rhs[s, j]
            stage(0, s, bs, PAD)
        start(fine(0, c))

    qall = jnp.where(row // 4 == lane % 32, 1.0 / 16.0, 0.0).astype(F32)

    def rows4(read):
        return read(0) + read(1) + read(2) + read(3)

    def every4(k):
        return pl.ds(k, cy, stride=4)

    cplanes = [rows4(lambda k, j=j: cond[j, every4(k), :]) for j in range(slots)]
    cplanes += [rows4(lambda k: klo[every4(k), :]), rows4(lambda k: khi[every4(k), :])]
    cmean = dot(jnp.concatenate(cplanes, axis=0), qall)
    cc = [cmean[j * cy:(j + 1) * cy] for j in range(slots + 2)]
    crow = lax.broadcasted_iota(jnp.int32, (cy, nz), 0)
    clane = lax.broadcasted_iota(jnp.int32, (cy, nz), 1) % 32
    for j in range(slots):
        c = cc[j]
        lo = cc[slots] if j == 0 else cc[j - 1]
        hi = jnp.where(n - 1 == j, cc[slots + 1], jnp.zeros_like(c) if j == slots - 1 else cc[j + 1])
        faces = [(c + lo) * 8.0, (c + hi) * 8.0,
                 (c + jnp.where(crow == 0, 0.0, pltpu.roll(c, 1, 0))) * 0.5,
                 (c + jnp.where(crow == cy - 1, 0.0, pltpu.roll(c, cy - 1, 0))) * 0.5,
                 (c + jnp.where(clane == 0, 0.0, pltpu.roll(c, 1, 1))) * 0.5,
                 (c + jnp.where(clane == 31, 0.0, pltpu.roll(c, nz - 1, 1))) * 0.5]
        diag = faces[0] + faces[1] + faces[2] + faces[3] + faces[4] + faces[5]
        scale = jnp.where(j < n, 1.0, 0.0) * (OMEGA / diag)
        cw[0, j] = scale * faces[0]
        cw[1, j] = scale * faces[1]
        cw[2, j] = jnp.where(crow == 0, 0.0, scale * faces[2])
        cw[3, j] = jnp.where(crow == cy - 1, 0.0, scale * faces[3])
        cw[4, j] = jnp.where(clane == 0, 0.0, scale * faces[4])
        cw[5, j] = jnp.where(clane == 31, 0.0, scale * faces[5])
        cwb[pl.ds(j * cy, cy), :] = scale

    def change(src, step, s, j, r0, wts, keep):
        o = PAD + r0
        rows = slice(o, o + RB)
        v = src[s, j, rows]
        nothing = jnp.zeros_like(v)
        if j > 0:
            lo = src[s, j - 1, rows]
        else:
            lo = nothing if step is None else hlo[step, s, r0:r0 + RB]
        edge_hi = nothing if step is None else hhi[step, s, r0:r0 + RB]
        above = jnp.zeros_like(edge_hi) if j == slots - 1 else src[s, j + 1, rows]
        hi = jnp.where(n - 1 == j, edge_hi, above)
        acc = bs[s, j, rows] + keep * v
        acc = acc + wts[0] * lo + wts[1] * hi
        acc = acc + wts[2] * src[s, j, o - 1:o - 1 + RB] + wts[3] * src[s, j, o + 1:o + 1 + RB]
        return acc + wts[4] * pltpu.roll(v, 1, 1) + wts[5] * pltpu.roll(v, nz - 1, 1)

    def weights(j, r0):
        return [w[i, j, r0:r0 + RB] for i in range(6)]

    def sweep(src, dst, off, step, prepare=None, ahead=chunks):
        @pl.loop(0, chunks)
        def _(c):
            if prepare is None:
                wait_recv(fine(step, c))
            else:
                prepare(c)
            for j in range(slots):
                for r0 in range(0, ny, RB):
                    wts = weights(j, r0)
                    for i in range(CH):
                        s = c * CH + i
                        dst[s, j, off + r0:off + r0 + RB] = change(
                            src, step, s, j, r0, wts, 1.0 - OMEGA)
            for i in range(CH):
                stage(step + 1, c * CH + i, dst, off)
            if step + 1 < STEPS - 1:
                @pl.when(c < ahead)
                def _():
                    start(fine(step + 1, c))
            else:
                first = c < chunks // 2

                @pl.when(first)
                def _():
                    start(fine(step + 1, c), dn=False)

                @pl.when(jnp.logical_not(first))
                def _():
                    start(fine(step + 1, c), up=False)

    def coarse_solve(src, step, k0, extra=None):
        cres[...] = jnp.zeros_like(cres)
        csup[k0] = jnp.zeros(csup.shape[1:], F32)
        csdn[k0] = jnp.zeros(csdn.shape[1:], F32)

        @pl.loop(0, chunks)
        def _(c):
            g = c // 2
            for i in range(CH):
                s = c * CH + i
                for j in range(slots):
                    for r0 in range(0, ny, RB):
                        rbuf[i, j, r0:r0 + RB] = dg[j, r0:r0 + RB] * change(
                            src, None, s, j, r0, weights(j, r0), -OMEGA)
                ebuf[i, 0] = fx[0] * sup[step, s]
                ebuf[i, 1] = fx[1] * sdn[step, s]
                sums = [rows4(lambda k, j=j: rbuf[i, j, every4(k), :]) for j in range(slots)]
                sums += [rows4(lambda k, e=e: ebuf[i, e, every4(k), :]) for e in range(2)]
                packed = dot(jnp.concatenate(sums, axis=0), qm[(c % 2) * CH + i])
                cres[g] = cres[g] + packed[:slots * cy]
                csup[k0, g] = csup[k0, g] + packed[slots * cy:(slots + 1) * cy]
                csdn[k0, g] = csdn[k0, g] + packed[(slots + 1) * cy:]

        start(coarse(k0))
        start(fine(step, 1))
        wait_recv(coarse(k0))

        for g in range(2):
            for j in range(slots):
                part = slice(j * cy, (j + 1) * cy)
                total = cres[g, part] + jnp.where(n - 1 == j, chhi[k0, g], 0.0)
                if j == 0:
                    total = total + chlo[k0, g]
                cbs[g, j] = cwb[part] * total
        for t in range(4):
            here = cbs if t == 0 else ce.at[t - 1]
            for g in range(2):
                csup[k0 + 1 + t, g] = here[g, top]
                csdn[k0 + 1 + t, g] = here[g, 0]
            start(coarse(k0 + 1 + t))
            if t + 2 < chunks:
                start(fine(step, t + 2))
            elif t == 2 and extra is not None:
                start(extra)
            if t < 3:
                wait_recv(coarse(k0 + 1 + t))
                for g in range(2):
                    for j in range(slots):
                        e = here[g, j]
                        lo = chlo[k0 + 1 + t, g] if j == 0 else here[g, j - 1]
                        above = jnp.zeros_like(e) if j == slots - 1 else here[g, j + 1]
                        hi = jnp.where(n - 1 == j, chhi[k0 + 1 + t, g], above)
                        ce[t, g, j] = (
                            cbs[g, j] + (1.0 - OMEGA) * e + cw[0, j] * lo + cw[1, j] * hi
                            + cw[2, j] * pltpu.roll(e, 1, 0) + cw[3, j] * pltpu.roll(e, cy - 1, 0)
                            + cw[4, j] * pltpu.roll(e, 1, 1) + cw[5, j] * pltpu.roll(e, nz - 1, 1))
        last = ce.at[2]
        wait_recv(coarse(k0 + 4))

        def add_correction(c):
            wait_recv(fine(step, c))
            g = c // 2
            packed = jnp.concatenate(
                [last[g, j] for j in range(slots)] + [chlo[k0 + 4, g], chhi[k0 + 4, g]], axis=0)
            for i in range(CH):
                s = c * CH + i
                wide = dot(packed, qt[(c % 2) * CH + i])
                for k in range(4):
                    for j in range(slots):
                        at = pl.ds(PAD + k, cy, stride=4)
                        src[s, j, at, :] = src[s, j, at, :] + wide[j * cy:(j + 1) * cy]
                    at = every4(k)
                    hlo[step, s, at, :] = hlo[step, s, at, :] + wide[slots * cy:(slots + 1) * cy]
                    hhi[step, s, at, :] = hhi[step, s, at, :] + wide[(slots + 1) * cy:]

        return add_correction

    sweep(bs, va, PAD, 0, ahead=1)
    correct = coarse_solve(va, 1, 0, fwd_pair)
    sweep(va, vb, PAD, 1, correct)
    sweep(vb, va, PAD, 2)
    sweep(va, vb, PAD, 3)
    sweep(vb, va, PAD, 4, ahead=1)
    correct = coarse_solve(va, 5, 5)
    sweep(va, vb, PAD, 5, correct)
    sweep(vb, adj, 0, 6)

    zero = jnp.zeros_like(sy)
    sy[...] = zero
    sz[...] = zero
    sfa[...] = zero
    sx[...] = zero

    @pl.loop(0, nsrc)
    def _(s):
        for j in range(slots):
            f, a = fwd[s, j], adj[s, j]
            sfa[j] = sfa[j] + f * a
            sy[j] = sy[j] + ((f - jnp.where(row == 0, 0.0, pltpu.roll(f, 1, 0)))
                             * (a - jnp.where(row == 0, 0.0, pltpu.roll(a, 1, 0))))
            sz[j] = sz[j] + ((f - jnp.where(lane == 0, 0.0, pltpu.roll(f, 1, 1)))
                             * (a - jnp.where(lane == 0, 0.0, pltpu.roll(a, 1, 1))))
            if j > 0:
                sx[j] = sx[j] + (f - fwd[s, j - 1]) * (a - adj[s, j - 1])

    wait_recv(fwd_pair)
    for c in range(chunks):
        wait_recv(fine(STEPS - 1, c), up=c < chunks // 2, dn=c >= chunks // 2)
    lower, upper = plane, plane
    for s in range(half):
        lower = lower + (fwd[s, 0] - fhlo[s]) * (adj[s, 0] - hlo[STEPS - 1, s])
    plo[...] = lower
    for s in range(half):
        upper = upper + ((fwd[half + s, top] - fhhi[s])
                         * (adj[half + s, top] - hhi[STEPS - 1, half + s]))
    phi[...] = upper
    start(prod_pair)

    @pl.when(jnp.logical_not(has_lo))
    def _():
        total = plane
        for s in range(half, nsrc):
            total = total + fwd[s, 0] * adj[s, 0]
        rlo[...] = total

    @pl.when(jnp.logical_not(has_hi))
    def _():
        total = plane
        for s in range(half):
            total = total + fwd[s, top] * adj[s, top]
        rhi[...] = total

    for j in range(slots):
        y_hi = jnp.where(row == ny - 1, sfa[j], pltpu.roll(sy[j], ny - 1, 0))
        z_hi = jnp.where(lane == nz - 1, sfa[j], pltpu.roll(sz[j], nz - 1, 1))
        sy[j] = sy[j] + y_hi + sz[j] + z_hi
    wait_recv(prod_pair)
    for j in range(slots):
        x_lo = plo[...] + rlo[...] if j == 0 else sx[j]
        x_hi = jnp.where(n - 1 == j, phi[...] + rhi[...], plane if j == slots - 1 else sx[j + 1])
        grad[j] = jnp.where(j < n, -0.5, 0.0) * (sy[j] + x_lo + x_hi)

    @pl.loop(0, STEPS - 1)
    def _(k):
        for c in range(chunks):
            wait_send(fine(k, c))
    for c in range(chunks):
        wait_send(fine(STEPS - 1, c), up=c < chunks // 2, dn=c >= chunks // 2)

    @pl.loop(0, CSTEPS)
    def _(k):
        wait_send(coarse(k))
    for pair in (cond_pair, fwd_pair, prod_pair):
        wait_send(pair)


def shards(conductivity, forward, adjoint_rhs, plane_counts):
    slots, ny, nz = conductivity.shape
    nsrc = forward.shape[0]
    half, chunks, cy = nsrc // 2, nsrc // CH, ny // 4
    vmem = functools.partial(pl.BlockSpec, memory_space=pltpu.VMEM)

    def buf(*shape):
        return pltpu.VMEM(shape, F32)

    def sems(*shape):
        return pltpu.SemaphoreType.DMA(shape)

    field = (nsrc, slots, ny + 2 * PAD, nz)
    scratch = [
        buf(7, slots, ny, nz), buf(slots, ny, nz), buf(*field), buf(*field), buf(*field),
        *[buf(STEPS, nsrc, ny, nz)] * 4,
        *[buf(half, ny, nz)] * 4,
        buf(4, nz, nz), buf(4, nz, nz),
        buf(6, slots, cy, nz), buf(slots * cy, nz), buf(2, slots * cy, nz),
        buf(2, slots, cy, nz), buf(3, 2, slots, cy, nz),
        *[buf(CSTEPS, 2, cy, nz)] * 4,
        *[buf(ny, nz)] * 8,
        *[buf(slots, ny, nz)] * 4,
        buf(CH, slots, ny, nz), buf(2, ny, nz), buf(CH, 2, ny, nz),
        *[sems(STEPS, chunks)] * 4,
        *[sems(CSTEPS)] * 4,
        *[sems(3)] * 4,
    ]
    return pl.pallas_call(
        kernel,
        out_shape=(jax.ShapeDtypeStruct(forward.shape, F32),
                   jax.ShapeDtypeStruct(conductivity.shape, F32)),
        in_specs=[pl.BlockSpec(memory_space=pltpu.SMEM), vmem(), vmem(), vmem()],
        out_specs=(vmem(), vmem()),
        scratch_shapes=scratch,
        compiler_params=pltpu.CompilerParams(
            collective_id=0, has_side_effects=True, vmem_limit_bytes=56 * 2**20),
    )(plane_counts, conductivity, forward, adjoint_rhs)


def solution(mesh):
    in_specs = (
        P("space", "groups", None),
        P("groups", "space", None, None),
        P("groups", "space", None, None),
        P("groups"),
    )
    out_specs = (P("groups", "space", None, None), P("space", "groups", None))
    return jax.shard_map(shards, mesh=mesh, in_specs=in_specs, out_specs=out_specs, check_vma=False)
```

```python
import functools

import jax
import jax.numpy as jnp
from jax import lax
from jax.experimental import pallas as pl
from jax.experimental.pallas import tpu as pltpu
from jax.sharding import PartitionSpec as P

OMEGA = 0.8
F32 = jnp.float32
PAD = 8
RB = 32
CH = 2
STEPS = 8
CSTEPS = 10


def dot(a, b):
    return jnp.dot(a, b, precision=lax.Precision.HIGHEST, preferred_element_type=F32)


def kernel(n_ref, cond, fwd, rhs, adj, grad,
           w, dg, bs, va, vb, hlo, hhi, sup, sdn, fhlo, fhhi, fsup, fsdn,
           qm, qt, cw, cwb, cres, cbs, ce, chlo, chhi, csup, csdn,
           kup, kdn, klo, khi, wup, wdn, wlo, whi, plo, phi, rlo, rhi, sy, sz, sfa, sx, rbuf, fx, ebuf,
           up_send, up_recv, dn_send, dn_recv, cup_send, cup_recv, cdn_send, cdn_recv,
           mup_send, mup_recv, mdn_send, mdn_recv):
    slots, ny, nz = cond.shape
    nsrc = fwd.shape[0]
    half = nsrc // 2
    chunks = nsrc // CH
    cy = ny // 4
    pos = lax.axis_index("space")
    peers = lax.axis_size("space")
    n = n_ref[pos]
    top = jnp.maximum(n - 1, 0)
    has_lo = pos > 0
    has_hi = pos < peers - 1

    def up_copy(src, dst, ss, rs):
        return pltpu.make_async_remote_copy(
            src_ref=src, dst_ref=dst, send_sem=ss, recv_sem=rs,
            device_id={"space": pos + 1}, device_id_type=pl.DeviceIdType.MESH)

    def dn_copy(src, dst, ss, rs):
        return pltpu.make_async_remote_copy(
            src_ref=src, dst_ref=dst, send_sem=ss, recv_sem=rs,
            device_id={"space": pos - 1}, device_id_type=pl.DeviceIdType.MESH)

    barrier = pltpu.get_barrier_semaphore()

    @pl.when(has_lo)
    def _():
        pl.semaphore_signal(barrier, inc=1, device_id={"space": pos - 1},
                            device_id_type=pl.DeviceIdType.MESH)

    @pl.when(has_hi)
    def _():
        pl.semaphore_signal(barrier, inc=1, device_id={"space": pos + 1},
                            device_id_type=pl.DeviceIdType.MESH)

    pl.semaphore_wait(barrier, jnp.where(has_lo, 1, 0) + jnp.where(has_hi, 1, 0))

    def fine(step, c):
        part = pl.ds(c * CH, CH)
        return (lambda: up_copy(sup.at[step, part], hlo.at[step, part],
                                up_send.at[step, c], up_recv.at[step, c]),
                lambda: dn_copy(sdn.at[step, part], hhi.at[step, part],
                                dn_send.at[step, c], dn_recv.at[step, c]))

    def coarse(k):
        return (lambda: up_copy(csup.at[k], chlo.at[k], cup_send.at[k], cup_recv.at[k]),
                lambda: dn_copy(csdn.at[k], chhi.at[k], cdn_send.at[k], cdn_recv.at[k]))

    def misc(i, us, ud, ds, dd):
        return (lambda: up_copy(us, ud, mup_send.at[i], mup_recv.at[i]),
                lambda: dn_copy(ds, dd, mdn_send.at[i], mdn_recv.at[i]))

    cond_pair = misc(0, kup, klo, kdn, khi)
    fwd_pair = misc(1, fsup, fhlo, fsdn, fhhi)
    scale_pair = misc(3, wup, wlo, wdn, whi)
    prod_pair = misc(2, phi, rlo, plo, rhi)

    def start(pair, up=True, dn=True):
        if up:
            @pl.when(has_hi)
            def _():
                pair[0]().start()
        if dn:
            @pl.when(has_lo)
            def _():
                pair[1]().start()

    def wait_recv(pair, up=True, dn=True):
        if up:
            @pl.when(has_lo)
            def _():
                pair[0]().wait_recv()
        if dn:
            @pl.when(has_hi)
            def _():
                pair[1]().wait_recv()

    def wait_send(pair, up=True, dn=True):
        if up:
            @pl.when(has_hi)
            def _():
                pair[0]().wait_send()
        if dn:
            @pl.when(has_lo)
            def _():
                pair[1]().wait_send()

    kup[...] = cond[top]
    kdn[...] = cond[0]
    start(cond_pair)

    for c in range(chunks):
        for i in range(CH):
            sup[0, c * CH + i] = rhs[c * CH + i, top]
            sdn[0, c * CH + i] = rhs[c * CH + i, 0]
        if c < chunks // 2:
            start(fine(0, c))

    plane = jnp.zeros((ny, nz), F32)

    @pl.when(jnp.logical_not(has_lo))
    def _():
        klo[...] = plane
        wlo[...] = plane
        chlo[...] = jnp.zeros_like(chlo)
        fhlo[...] = jnp.zeros_like(fhlo)

        @pl.loop(0, STEPS)
        def _(k):
            hlo[k] = jnp.zeros(hlo.shape[1:], F32)

    @pl.when(jnp.logical_not(has_hi))
    def _():
        khi[...] = plane
        whi[...] = plane
        chhi[...] = jnp.zeros_like(chhi)
        fhhi[...] = jnp.zeros_like(fhhi)

        @pl.loop(0, STEPS)
        def _(k):
            hhi[k] = jnp.zeros(hhi.shape[1:], F32)

    edge = jnp.zeros((slots, PAD, nz), F32)

    @pl.loop(0, nsrc)
    def _(s):
        for buf in (bs, va, vb):
            buf[s, :, :PAD] = edge
            buf[s, :, PAD + ny:] = edge

    row = lax.broadcasted_iota(jnp.int32, (ny, nz), 0)
    lane = lax.broadcasted_iota(jnp.int32, (ny, nz), 1)
    for s4 in range(4):
        qm[s4] = jnp.where(row // 4 + 32 * s4 == lane, 1.0, 0.0).astype(F32)
        qt[s4] = jnp.where(lane // 4 + 32 * s4 == row, 1.0, 0.0).astype(F32)

    @pl.loop(0, half)
    def _(s):
        fsup[s] = fwd[s, top]
        fsdn[s] = fwd[half + s, 0]

    wait_recv(cond_pair)
    fx[0] = (cond[top] + khi[...]) * 0.5
    fx[1] = (cond[0] + klo[...]) * 0.5

    for j in range(slots):
        c = cond[j]
        lo = klo[...] if j == 0 else cond[j - 1]
        above = plane if j == slots - 1 else cond[j + 1]
        hi = jnp.where(n - 1 == j, khi[...], above)
        faces = [(c + lo) * 0.5, (c + hi) * 0.5,
                 (c + jnp.where(row == 0, 0.0, pltpu.roll(c, 1, 0))) * 0.5,
                 (c + jnp.where(row == ny - 1, 0.0, pltpu.roll(c, ny - 1, 0))) * 0.5,
                 (c + jnp.where(lane == 0, 0.0, pltpu.roll(c, 1, 1))) * 0.5,
                 (c + jnp.where(lane == nz - 1, 0.0, pltpu.roll(c, nz - 1, 1))) * 0.5]
        diag = faces[0] + faces[1] + faces[2] + faces[3] + faces[4] + faces[5]
        alive = jnp.where(j < n, 1.0, 0.0)
        scale = alive * (OMEGA / diag)
        dg[j] = alive * diag * (1.0 / OMEGA)
        for i in range(4):
            w[i, j] = scale * faces[i]
        w[4, j] = jnp.where(lane == 0, 0.0, scale * faces[4])
        w[5, j] = jnp.where(lane == nz - 1, 0.0, scale * faces[5])
        w[6, j] = scale

    def stage(step, s, buf, off):
        sup[step, s] = buf[s, top, off:off + ny]
        sdn[step, s] = buf[s, 0, off:off + ny]

    wup[...] = w[6, top]
    wdn[...] = w[6, 0]
    start(scale_pair)
    for c in range(chunks // 2, chunks):
        start(fine(0, c))

    @pl.loop(0, chunks)
    def _(c):
        for i in range(CH):
            s = c * CH + i
            for j in range(slots):
                bs[s, j, PAD:PAD + ny] = w[6, j] * rhs[s, j]

    qall = jnp.where(row // 4 == lane % 32, 1.0 / 16.0, 0.0).astype(F32)

    def rows4(read):
        return read(0) + read(1) + read(2) + read(3)

    def every4(k):
        return pl.ds(k, cy, stride=4)

    cplanes = [rows4(lambda k, j=j: cond[j, every4(k), :]) for j in range(slots)]
    cplanes += [rows4(lambda k: klo[every4(k), :]), rows4(lambda k: khi[every4(k), :])]
    cmean = dot(jnp.concatenate(cplanes, axis=0), qall)
    cc = [cmean[j * cy:(j + 1) * cy] for j in range(slots + 2)]
    crow = lax.broadcasted_iota(jnp.int32, (cy, nz), 0)
    clane = lax.broadcasted_iota(jnp.int32, (cy, nz), 1) % 32
    for j in range(slots):
        c = cc[j]
        lo = cc[slots] if j == 0 else cc[j - 1]
        hi = jnp.where(n - 1 == j, cc[slots + 1], jnp.zeros_like(c) if j == slots - 1 else cc[j + 1])
        faces = [(c + lo) * 8.0, (c + hi) * 8.0,
                 (c + jnp.where(crow == 0, 0.0, pltpu.roll(c, 1, 0))) * 0.5,
                 (c + jnp.where(crow == cy - 1, 0.0, pltpu.roll(c, cy - 1, 0))) * 0.5,
                 (c + jnp.where(clane == 0, 0.0, pltpu.roll(c, 1, 1))) * 0.5,
                 (c + jnp.where(clane == 31, 0.0, pltpu.roll(c, nz - 1, 1))) * 0.5]
        diag = faces[0] + faces[1] + faces[2] + faces[3] + faces[4] + faces[5]
        scale = jnp.where(j < n, 1.0, 0.0) * (OMEGA / diag)
        cw[0, j] = scale * faces[0]
        cw[1, j] = scale * faces[1]
        cw[2, j] = jnp.where(crow == 0, 0.0, scale * faces[2])
        cw[3, j] = jnp.where(crow == cy - 1, 0.0, scale * faces[3])
        cw[4, j] = jnp.where(clane == 0, 0.0, scale * faces[4])
        cw[5, j] = jnp.where(clane == 31, 0.0, scale * faces[5])
        cwb[pl.ds(j * cy, cy), :] = scale

    def change(src, step, s, j, r0, wts, keep):
        o = PAD + r0
        rows = slice(o, o + RB)
        v = src[s, j, rows]
        nothing = jnp.zeros_like(v)
        if j > 0:
            lo = src[s, j - 1, rows]
        else:
            lo = nothing if step is None else hlo[step, s, r0:r0 + RB]
        edge_hi = nothing if step is None else hhi[step, s, r0:r0 + RB]
        above = jnp.zeros_like(edge_hi) if j == slots - 1 else src[s, j + 1, rows]
        hi = jnp.where(n - 1 == j, edge_hi, above)
        acc = bs[s, j, rows] + keep * v
        acc = acc + wts[0] * lo + wts[1] * hi
        acc = acc + wts[2] * src[s, j, o - 1:o - 1 + RB] + wts[3] * src[s, j, o + 1:o + 1 + RB]
        return acc + wts[4] * pltpu.roll(v, 1, 1) + wts[5] * pltpu.roll(v, nz - 1, 1)

    def weights(j, r0):
        return [w[i, j, r0:r0 + RB] for i in range(6)]

    def sweep(src, dst, off, step, prepare=None, ahead=chunks):
        @pl.loop(0, chunks)
        def _(c):
            if prepare is None:
                wait_recv(fine(step, c))
            else:
                prepare(c)
            for j in range(slots):
                for r0 in range(0, ny, RB):
                    wts = weights(j, r0)
                    for i in range(CH):
                        s = c * CH + i
                        dst[s, j, off + r0:off + r0 + RB] = change(
                            src, step, s, j, r0, wts, 1.0 - OMEGA)
            for i in range(CH):
                stage(step + 1, c * CH + i, dst, off)
            if step + 1 < STEPS - 1:
                @pl.when(c < ahead)
                def _():
                    start(fine(step + 1, c))
            else:
                first = c < chunks // 2

                @pl.when(first)
                def _():
                    start(fine(step + 1, c), dn=False)

                @pl.when(jnp.logical_not(first))
                def _():
                    start(fine(step + 1, c), up=False)

    def coarse_solve(src, step, k0, extra=None):
        cres[...] = jnp.zeros_like(cres)
        csup[k0] = jnp.zeros(csup.shape[1:], F32)
        csdn[k0] = jnp.zeros(csdn.shape[1:], F32)

        @pl.loop(0, chunks)
        def _(c):
            g = c // 2
            for i in range(CH):
                s = c * CH + i
                for j in range(slots):
                    for r0 in range(0, ny, RB):
                        rbuf[i, j, r0:r0 + RB] = dg[j, r0:r0 + RB] * change(
                            src, None, s, j, r0, weights(j, r0), -OMEGA)
                ebuf[i, 0] = fx[0] * sup[step, s]
                ebuf[i, 1] = fx[1] * sdn[step, s]
                sums = [rows4(lambda k, j=j: rbuf[i, j, every4(k), :]) for j in range(slots)]
                sums += [rows4(lambda k, e=e: ebuf[i, e, every4(k), :]) for e in range(2)]
                packed = dot(jnp.concatenate(sums, axis=0), qm[(c % 2) * CH + i])
                cres[g] = cres[g] + packed[:slots * cy]
                csup[k0, g] = csup[k0, g] + packed[slots * cy:(slots + 1) * cy]
                csdn[k0, g] = csdn[k0, g] + packed[(slots + 1) * cy:]

        start(coarse(k0))
        start(fine(step, 1))
        wait_recv(coarse(k0))

        for g in range(2):
            for j in range(slots):
                part = slice(j * cy, (j + 1) * cy)
                total = cres[g, part] + jnp.where(n - 1 == j, chhi[k0, g], 0.0)
                if j == 0:
                    total = total + chlo[k0, g]
                cbs[g, j] = cwb[part] * total
        for t in range(4):
            here = cbs if t == 0 else ce.at[t - 1]
            for g in range(2):
                csup[k0 + 1 + t, g] = here[g, top]
                csdn[k0 + 1 + t, g] = here[g, 0]
            start(coarse(k0 + 1 + t))
            if t + 2 < chunks:
                start(fine(step, t + 2))
            elif t == 2 and extra is not None:
                start(extra)
            if t < 3:
                wait_recv(coarse(k0 + 1 + t))
                for g in range(2):
                    for j in range(slots):
                        e = here[g, j]
                        lo = chlo[k0 + 1 + t, g] if j == 0 else here[g, j - 1]
                        above = jnp.zeros_like(e) if j == slots - 1 else here[g, j + 1]
                        hi = jnp.where(n - 1 == j, chhi[k0 + 1 + t, g], above)
                        ce[t, g, j] = (
                            cbs[g, j] + (1.0 - OMEGA) * e + cw[0, j] * lo + cw[1, j] * hi
                            + cw[2, j] * pltpu.roll(e, 1, 0) + cw[3, j] * pltpu.roll(e, cy - 1, 0)
                            + cw[4, j] * pltpu.roll(e, 1, 1) + cw[5, j] * pltpu.roll(e, nz - 1, 1))
        last = ce.at[2]
        wait_recv(coarse(k0 + 4))

        def add_correction(c):
            wait_recv(fine(step, c))
            g = c // 2
            packed = jnp.concatenate(
                [last[g, j] for j in range(slots)] + [chlo[k0 + 4, g], chhi[k0 + 4, g]], axis=0)
            for i in range(CH):
                s = c * CH + i
                wide = dot(packed, qt[(c % 2) * CH + i])
                for k in range(4):
                    for j in range(slots):
                        at = pl.ds(PAD + k, cy, stride=4)
                        src[s, j, at, :] = src[s, j, at, :] + wide[j * cy:(j + 1) * cy]
                    at = every4(k)
                    hlo[step, s, at, :] = hlo[step, s, at, :] + wide[slots * cy:(slots + 1) * cy]
                    hhi[step, s, at, :] = hhi[step, s, at, :] + wide[(slots + 1) * cy:]

        return add_correction

    wait_recv(scale_pair)

    def scale_planes(c):
        wait_recv(fine(0, c))
        for i in range(CH):
            s = c * CH + i
            hlo[0, s] = hlo[0, s] * wlo[...]
            hhi[0, s] = hhi[0, s] * whi[...]

    sweep(bs, va, PAD, 0, scale_planes, ahead=1)
    correct = coarse_solve(va, 1, 0, fwd_pair)
    sweep(va, vb, PAD, 1, correct)
    sweep(vb, va, PAD, 2)
    sweep(va, vb, PAD, 3)
    sweep(vb, va, PAD, 4, ahead=1)
    correct = coarse_solve(va, 5, 5)
    sweep(va, vb, PAD, 5, correct)
    sweep(vb, adj, 0, 6)

    zero = jnp.zeros_like(sy)
    sy[...] = zero
    sz[...] = zero
    sfa[...] = zero
    sx[...] = zero

    @pl.loop(0, nsrc)
    def _(s):
        for j in range(slots):
            f, a = fwd[s, j], adj[s, j]
            sfa[j] = sfa[j] + f * a
            sy[j] = sy[j] + ((f - jnp.where(row == 0, 0.0, pltpu.roll(f, 1, 0)))
                             * (a - jnp.where(row == 0, 0.0, pltpu.roll(a, 1, 0))))
            sz[j] = sz[j] + ((f - jnp.where(lane == 0, 0.0, pltpu.roll(f, 1, 1)))
                             * (a - jnp.where(lane == 0, 0.0, pltpu.roll(a, 1, 1))))
            if j > 0:
                sx[j] = sx[j] + (f - fwd[s, j - 1]) * (a - adj[s, j - 1])

    wait_recv(fwd_pair)
    for c in range(chunks):
        wait_recv(fine(STEPS - 1, c), up=c < chunks // 2, dn=c >= chunks // 2)
    lower, upper = plane, plane
    for s in range(half):
        lower = lower + (fwd[s, 0] - fhlo[s]) * (adj[s, 0] - hlo[STEPS - 1, s])
    plo[...] = lower
    for s in range(half):
        upper = upper + ((fwd[half + s, top] - fhhi[s])
                         * (adj[half + s, top] - hhi[STEPS - 1, half + s]))
    phi[...] = upper
    start(prod_pair)

    @pl.when(jnp.logical_not(has_lo))
    def _():
        total = plane
        for s in range(half, nsrc):
            total = total + fwd[s, 0] * adj[s, 0]
        rlo[...] = total

    @pl.when(jnp.logical_not(has_hi))
    def _():
        total = plane
        for s in range(half):
            total = total + fwd[s, top] * adj[s, top]
        rhi[...] = total

    for j in range(slots):
        y_hi = jnp.where(row == ny - 1, sfa[j], pltpu.roll(sy[j], ny - 1, 0))
        z_hi = jnp.where(lane == nz - 1, sfa[j], pltpu.roll(sz[j], nz - 1, 1))
        sy[j] = sy[j] + y_hi + sz[j] + z_hi
    wait_recv(prod_pair)
    for j in range(slots):
        x_lo = plo[...] + rlo[...] if j == 0 else sx[j]
        x_hi = jnp.where(n - 1 == j, phi[...] + rhi[...], plane if j == slots - 1 else sx[j + 1])
        grad[j] = jnp.where(j < n, -0.5, 0.0) * (sy[j] + x_lo + x_hi)

    @pl.loop(0, STEPS - 1)
    def _(k):
        for c in range(chunks):
            wait_send(fine(k, c))
    for c in range(chunks):
        wait_send(fine(STEPS - 1, c), up=c < chunks // 2, dn=c >= chunks // 2)

    @pl.loop(0, CSTEPS)
    def _(k):
        wait_send(coarse(k))
    for pair in (cond_pair, fwd_pair, prod_pair, scale_pair):
        wait_send(pair)


def shards(conductivity, forward, adjoint_rhs, plane_counts):
    slots, ny, nz = conductivity.shape
    nsrc = forward.shape[0]
    half, chunks, cy = nsrc // 2, nsrc // CH, ny // 4
    vmem = functools.partial(pl.BlockSpec, memory_space=pltpu.VMEM)

    def buf(*shape):
        return pltpu.VMEM(shape, F32)

    def sems(*shape):
        return pltpu.SemaphoreType.DMA(shape)

    field = (nsrc, slots, ny + 2 * PAD, nz)
    scratch = [
        buf(7, slots, ny, nz), buf(slots, ny, nz), buf(*field), buf(*field), buf(*field),
        *[buf(STEPS, nsrc, ny, nz)] * 4,
        *[buf(half, ny, nz)] * 4,
        buf(4, nz, nz), buf(4, nz, nz),
        buf(6, slots, cy, nz), buf(slots * cy, nz), buf(2, slots * cy, nz),
        buf(2, slots, cy, nz), buf(3, 2, slots, cy, nz),
        *[buf(CSTEPS, 2, cy, nz)] * 4,
        *[buf(ny, nz)] * 12,
        *[buf(slots, ny, nz)] * 4,
        buf(CH, slots, ny, nz), buf(2, ny, nz), buf(CH, 2, ny, nz),
        *[sems(STEPS, chunks)] * 4,
        *[sems(CSTEPS)] * 4,
        *[sems(4)] * 4,
    ]
    return pl.pallas_call(
        kernel,
        out_shape=(jax.ShapeDtypeStruct(forward.shape, F32),
                   jax.ShapeDtypeStruct(conductivity.shape, F32)),
        in_specs=[pl.BlockSpec(memory_space=pltpu.SMEM), vmem(), vmem(), vmem()],
        out_specs=(vmem(), vmem()),
        scratch_shapes=scratch,
        compiler_params=pltpu.CompilerParams(
            collective_id=0, has_side_effects=True, vmem_limit_bytes=56 * 2**20),
    )(plane_counts, conductivity, forward, adjoint_rhs)


def solution(mesh):
    in_specs = (
        P("space", "groups", None),
        P("groups", "space", None, None),
        P("groups", "space", None, None),
        P("groups"),
    )
    out_specs = (P("groups", "space", None, None), P("space", "groups", None))
    return jax.shard_map(shards, mesh=mesh, in_specs=in_specs, out_specs=out_specs, check_vma=False)
```
